32 devices in a mesh: mp: 2 (over x), dp: 4 (over y, core), tensor: 4 (over z).
Axes of the slice: x: 2, y: 2, z: 4, core: 2. Of those that a mesh axis runs over, the one named last changes fastest.
Arguments:
- activations: bfloat16 [2, 512, 8192], P('mp', 'dp'), may hold values from -6 to 6
- gate_pre: bfloat16 [2, 512, 28672], P('mp', 'dp', 'tensor'), may hold values from -6 to 6
- hidden_grad: bfloat16 [2, 512, 28672], P('mp', 'dp', 'tensor'), may hold values from -1.2 to 1.2, as said below
- up_weights: bfloat16 [2, 8192, 28672], P('mp', 'dp', 'tensor'), may hold values from -6 to 6
Outputs:
- merged: bfloat16 [8192, 28672], P(('dp', 'mp'), 'tensor')
The draws below stay inside these ranges and needn't reach their ends.
Inputs may be any that keep to these rules, and one draw needn't show every extreme that they name: `hidden_grad`: each sequence's values share one scale, spread evenly in the logarithm between 0.005 and 0.3 over sequences.
All inputs are finite; a program needn't handle non-finite values.
Results may differ from the reference program's by a relative error of at most 0.003.
Values may be sent and summed in bfloat16 or wider, within the bound.
A program may use at most 320 MiB of HBM per device.

```python
import math
import jax
import jax.numpy as jnp
from jax import lax

D = 8192
FF = 28672
LEN = 128
SEQS = 4
TOKENS = 512
MODELS = 2
N_TENSOR = 4


def draw_activations(key, part):
    key_common = jax.random.fold_in(key, 31)
    key_own = jax.random.fold_in(key, 37)
    common = jax.random.normal(key_common, (MODELS, SEQS, 1, D), jnp.float32)
    own = jax.random.normal(key_own, (MODELS, SEQS, LEN, D), jnp.float32)
    base = 0.8 * common + 0.6 * own
    values = jnp.clip(base, -6.0, 6.0).reshape(MODELS, SEQS * LEN, D)
    return values.astype(jnp.bfloat16)


def draw_hidden_grad(key, part):
    key_scale = jax.random.fold_in(key, 11)
    key_base = jax.random.fold_in(key, 23)
    key_common = jax.random.fold_in(key, 29)
    scales = jnp.exp(jax.random.uniform(key_scale, (MODELS, SEQS, 1, 1), jnp.float32, math.log(0.005), math.log(0.3)))
    common = jax.random.normal(key_common, (MODELS, SEQS, 1, FF), jnp.float32)
    own = jax.random.normal(key_base, (MODELS, SEQS, LEN, FF), jnp.float32)
    base = 0.8 * common + 0.6 * own
    values = (scales * jnp.clip(base, -4.0, 4.0)).reshape(MODELS, SEQS * LEN, FF)
    return values.astype(jnp.bfloat16)


def levels(stream_key, extent, split, least, largest):
    def one(position, blocks):
        steps = jax.random.uniform(jax.random.fold_in(jax.random.fold_in(stream_key, 6), position), (blocks,), jnp.float32, least / len(split), largest / len(split))
        return jnp.repeat(jnp.exp(steps), extent[position] // blocks).reshape((-1,) + (1,) * (len(extent) - position - 1))

    loudness = one(*split[0])
    for cut in split[1:]:
        loudness = loudness * one(*cut)
    return loudness


def scatter_about(key, extent, deviation, most, shards=(), kind=jnp.bfloat16):
    level = levels(key, extent, shards, -0.22, 0.18) if shards else 1.0
    array = jax.random.normal(key, extent, jnp.float32) * deviation * level
    return jnp.minimum(jnp.maximum(array, -most), most).astype(kind)


def setup_inputs(seed: int = 0) -> dict:
    key_list = jax.random.split(jax.random.key(seed), 5)
    activations = draw_activations(jax.random.fold_in(key_list[4], 71), 0)
    gate_pre = scatter_about(key_list[1], (MODELS, TOKENS, FF), 1.0, 6.0, ((0, 2), (1, 4), (2, 4)))
    hidden_grad = draw_hidden_grad(jax.random.fold_in(key_list[4], 71), 0)
    up_weights = scatter_about(key_list[3], (MODELS, D, FF), 1.0, 6.0, ((0, 2), (1, 4), (2, 4)))
    return {"activations": activations, "gate_pre": gate_pre, "hidden_grad": hidden_grad, "up_weights": up_weights}


clip_ratio = 0.05
fisher_floor = 0.1

def reference(activations, gate_pre, hidden_grad, up_weights):
    single_precision = jnp.float32
    cot_low = lax.optimization_barrier((hidden_grad.astype(single_precision) * jax.nn.silu(gate_pre.astype(single_precision))).astype(jnp.bfloat16))
    cot_seq = cot_low.astype(single_precision).reshape(MODELS, SEQS, LEN, FF)
    sequence_inputs = activations.astype(single_precision).reshape(MODELS, SEQS, LEN, D)
    input_gram_matrix = jnp.einsum('msld,msnd->msln', sequence_inputs, sequence_inputs)
    gram_cot = jnp.einsum('mslf,msnf->msln', cot_seq, cot_seq)
    grad_norm = jnp.sqrt(lax.optimization_barrier(jnp.sum(input_gram_matrix * gram_cot, axis=(2, 3))))
    clip_limit = clip_ratio * (LEN * D * FF) ** 0.5
    factor = clip_limit / jnp.maximum(grad_norm, clip_limit)
    clip_sq = factor * factor
    block = FF // N_TENSOR

    def column_block(index):
        begin = (index * block).astype(jnp.int32)
        columns = lax.dynamic_slice_in_dim(cot_seq, begin, block, 3)
        weight_cols = lax.dynamic_slice_in_dim(up_weights, begin, block, 2).astype(single_precision)

        def add_seq(total, seq_index):
            grad = jnp.einsum('mld,mlf->mdf', sequence_inputs[:, seq_index], columns[:, seq_index])
            return (total + clip_sq[:, seq_index, None, None] * grad * grad, None)
        fisher, unused = lax.scan(add_seq, jnp.zeros((MODELS, D, block), single_precision), jnp.arange(SEQS, dtype=jnp.int32))
        weighted = fisher + fisher_floor
        return (lax.optimization_barrier(jnp.sum(weighted * weight_cols, axis=0)) / lax.optimization_barrier(jnp.sum(weighted, axis=0))).astype(jnp.bfloat16)
    stacked = lax.map(column_block, jnp.arange(N_TENSOR, dtype=jnp.int32))
    return jnp.transpose(stacked, (1, 0, 2)).reshape(D, FF)
```

```python
import functools
import math

import jax
import jax.numpy as jnp
from jax import lax
from jax.experimental import pallas as pl
from jax.experimental.pallas import tpu as pltpu
from jax.sharding import PartitionSpec as P

LEN = 128
CORES = 2
PIECES = 16
AHEAD = 8
clip_ratio = 0.05
fisher_floor = 0.1
f32 = jnp.float32
bf16 = jnp.bfloat16


def kernel(
    sizes, acts_ref, gate_ref, hid_ref, w_ref, out_ref,
    acts, acts_t, gate, hid, cot, cols_in, w_far, w_own, ratio, merged, part, clips,
    load_sem, own_sem, out_sem,
    w_send, w_recv, c_send, c_recv, a_send, a_recv, z_send, z_recv, k_send, k_recv,
):
    models, seqs, slices = sizes
    m, d, t = lax.axis_index("mp"), lax.axis_index("dp"), lax.axis_index("tensor")
    other = 1 - m
    ys = seqs // CORES
    y, core = d // CORES, d % CORES
    mate = y * CORES + (1 - core)
    width, ff = acts.shape[1], gate.shape[1]
    keep = w_far.shape[0]
    piece = keep // PIECES
    chunk = 2 * piece
    chunks = PIECES // 2
    tile = math.gcd(ff, 512)

    def place(where):
        return dict(zip(("mp", "dp", "tensor"), where))

    def push(src, dst, send, recv, where):
        return pltpu.make_async_remote_copy(
            src_ref=src, dst_ref=dst, send_sem=send, recv_sem=recv,
            device_id=place(where), device_id_type=pl.DeviceIdType.MESH,
        )

    def rest(offset):
        return [(a, b) for a in range(models) for b in range(seqs) if a or b][offset:]

    def plane(a, b):
        return lax.rem(m + a, models), lax.rem(d + b, seqs)

    loads = [
        pltpu.make_async_copy(src, dst, load_sem.at[i])
        for i, (src, dst) in enumerate(((gate_ref, gate), (hid_ref, hid), (acts_ref, acts)))
    ]
    for copy in loads:
        copy.start()

    barrier = pltpu.get_barrier_semaphore()
    for a, b in rest(0):
        pm, pd = plane(a, b)
        pl.semaphore_signal(barrier, inc=1, device_id=place((pm, pd, t)), device_id_type=pl.DeviceIdType.MESH)
    for o in range(1, slices):
        pl.semaphore_signal(
            barrier, inc=1, device_id=place((m, d, lax.rem(t + o, slices))), device_id_type=pl.DeviceIdType.MESH
        )
    pl.semaphore_wait(barrier, models * seqs - 1 + slices - 1)

    def w_piece(k):
        return push(
            w_ref.at[pl.ds(pl.multiple_of(other * keep + k * piece, piece), piece), :],
            w_far.at[pl.ds(pl.multiple_of(k * piece, piece), piece), :],
            w_send.at[k], w_recv.at[k], (other, d, t),
        )

    for k in range(2):
        w_piece(k).start()

    def own_chunk(i):
        slot = lax.rem(i, 2)
        return pltpu.make_async_copy(
            w_ref.at[pl.ds(pl.multiple_of(m * keep + i * chunk, chunk), chunk), :],
            w_own.at[slot], own_sem.at[slot],
        )

    own_chunk(0).start()

    loads[0].wait()
    loads[1].wait()

    @pl.loop(0, ff // tile)
    def _(j):
        at = pl.ds(pl.multiple_of(j * tile, tile), tile)
        v = gate[:, at].astype(f32)
        cot[m, d, :, at] = (hid[:, at].astype(f32) * (v / (1.0 + jnp.exp(-v)))).astype(bf16)

    def cot_to(cm, cs, kind, where):
        return push(cot.at[cm, cs], cot.at[cm, cs], c_send.at[cm, cs, kind], c_recv.at[cm, cs], where)

    def along_y(cm, cs):
        return [cot_to(cm, cs, 1 + o, (m, lax.rem(y + o, ys) * CORES + core, t)) for o in range(1, ys)]

    across = cot_to(m, d, 0, (other, d, t))
    first = [across] + along_y(m, d) + [cot_to(m, d, 1, (m, mate, t))]
    for copy in first:
        copy.start()

    loads[2].wait()
    step = math.gcd(width, 512)

    @pl.loop(0, width // step)
    def _(j):
        at = pl.ds(pl.multiple_of(j * step, step), step)
        acts_t[at, :] = acts[:, at].T

    def block(bm, bd):
        return acts_t.at[pl.ds(pl.multiple_of((bd * models + bm) * keep, keep), keep), :]

    blocks = []
    for a, b in rest(0):
        pm, pd = plane(a, b)
        blocks.append(push(block(pm, pd), cols_in.at[m, d], a_send.at[a, b], a_recv.at[m, d], (pm, pd, t)))
    for copy in blocks:
        copy.start()
    for k in range(2, 4):
        w_piece(k).start()
    cols_in[m, d] = block(m, d)[...]

    def gram(ref, lead, size):
        deep = math.gcd(size, 1024)

        def add(j, total):
            at = pl.ds(pl.multiple_of(j * deep, deep), deep)
            x = ref[:, at] if lead is None else ref[lead[0], lead[1], :, at]
            return total + lax.dot_general(x, x, (((1,), (1,)), ((), ())), preferred_element_type=f32)

        return lax.fori_loop(0, size // deep, add, jnp.zeros((LEN, LEN), f32))

    share = jnp.sum(gram(acts, None, width) * gram(cot, (m, d), ff), axis=(0, 1), keepdims=True)
    part[t] = jnp.broadcast_to(share, part.shape[1:])
    shares = [
        push(part.at[t], part.at[t], z_send.at[o], z_recv.at[t], (m, d, lax.rem(t + o, slices)))
        for o in range(1, slices)
    ]
    for copy in shares:
        copy.start()
    for o in range(1, slices):
        f = lax.rem(t + o, slices)
        push(part.at[f], part.at[f], z_send.at[o], z_recv.at[f], (m, d, f)).wait_recv()
    norm = jnp.sqrt(jnp.sum(part[...], axis=0))
    limit = clip_ratio * math.sqrt(LEN * width * ff * slices)
    factor = limit / jnp.maximum(norm, limit)
    clips[m, d] = factor * factor
    factors = []
    for a, b in rest(0):
        pm, pd = plane(a, b)
        factors.append(push(clips.at[m, d], clips.at[m, d], k_send.at[a, b], k_recv.at[m, d], (pm, pd, t)))
    for copy in factors:
        copy.start()

    def arrived(cm, cs):
        cot_to(cm, cs, 0, (other, d, t)).wait_recv()

    arrived(other, d)
    second = along_y(other, d) + [cot_to(other, d, 1, (m, mate, t))]
    for copy in second:
        copy.start()
    for k in range(4, AHEAD):
        w_piece(k).start()
    third = []
    for cm in (m, other):
        for o in range(1, ys):
            cs = lax.rem(y + o, ys) * CORES + core
            arrived(cm, cs)
            copy = cot_to(cm, cs, 1, (m, mate, t))
            copy.start()
            third.append(copy)
    for cm in (m, other):
        for o in range(ys):
            arrived(cm, lax.rem(y + o, ys) * CORES + (1 - core))
    for a, b in rest(0):
        pm, pd = plane(a, b)
        push(block(pm, pd), cols_in.at[pm, pd], a_send.at[a, b], a_recv.at[pm, pd], (pm, pd, t)).wait_recv()
        push(clips.at[pm, pd], clips.at[pm, pd], k_send.at[a, b], k_recv.at[pm, pd], (pm, pd, t)).wait_recv()

    def out_chunk(i):
        slot = lax.rem(i, 2)
        return pltpu.make_async_copy(
            merged.at[slot], out_ref.at[pl.ds(pl.multiple_of(i * chunk, chunk), chunk), :], out_sem.at[slot]
        )

    @pl.loop(0, chunks)
    def _(i):
        slot = lax.rem(i, 2)
        rows = pl.ds(pl.multiple_of(i * chunk, chunk), chunk)

        @pl.when(i >= 1)
        def _():
            w_piece(2 * i - 2).wait_send()
            w_piece(2 * i - 1).wait_send()

        @pl.when((2 * i + 2 >= AHEAD) & (2 * i + 2 < PIECES))
        def _():
            w_piece(2 * i + 2).start()
            w_piece(2 * i + 3).start()

        @pl.when(i + 1 < chunks)
        def _():
            own_chunk(i + 1).start()

        @pl.loop(0, ff // tile)
        def _(j):
            at = pl.ds(pl.multiple_of(j * tile, tile), tile)

            def weight(fm):
                total = jnp.full((chunk, tile), fisher_floor, f32)
                fisher = None
                for s in range(seqs):
                    grad = jnp.dot(cols_in[fm, s, rows, :], cot[fm, s, :, at], preferred_element_type=f32)
                    term = clips[fm, s, 0:1, 0:1] * (grad * grad)
                    fisher = term if fisher is None else fisher + term
                return fisher + total

            far = weight(other)
            ratio[:, at] = far / (far + weight(m))

        own_chunk(i).wait()

        @pl.when(i >= 2)
        def _():
            out_chunk(i - 2).wait()

        w_piece(2 * i).wait_recv()
        w_piece(2 * i + 1).wait_recv()

        @pl.loop(0, ff // tile)
        def _(j):
            at = pl.ds(pl.multiple_of(j * tile, tile), tile)
            near = w_own[slot, :, at].astype(f32)
            far = w_far[rows, at].astype(f32)
            merged[slot, :, at] = (near + ratio[:, at] * (far - near)).astype(bf16)

        out_chunk(i).start()

    for k in range(PIECES - 2, PIECES):
        w_piece(k).wait_send()
    for copy in first + second + third + blocks + shares + factors:
        copy.wait_send()
    for i in range(chunks - 2, chunks):
        out_chunk(i).wait()


def solution(mesh):
    models, seqs, slices = mesh.shape["mp"], mesh.shape["dp"], mesh.shape["tensor"]

    def local(activations, gate_pre, hidden_grad, up_weights):
        tokens, width = activations.shape[1:]
        ff = gate_pre.shape[2]
        keep = up_weights.shape[1] // models
        chunk = keep // PIECES * 2
        assert tokens == LEN and models == 2 and seqs % CORES == 0
        dma, vmem = pltpu.SemaphoreType.DMA, pltpu.VMEM
        return pl.pallas_call(
            functools.partial(kernel, (models, seqs, slices)),
            out_shape=jax.ShapeDtypeStruct((keep, ff), bf16),
            in_specs=[pl.BlockSpec(memory_space=pl.ANY)] * 4,
            out_specs=pl.BlockSpec(memory_space=pl.ANY),
            scratch_shapes=[
                vmem((LEN, width), bf16),
                vmem((width, LEN), bf16),
                vmem((LEN, ff), bf16),
                vmem((LEN, ff), bf16),
                vmem((models, seqs, LEN, ff), bf16),
                vmem((models, seqs, keep, LEN), bf16),
                vmem((keep, ff), bf16),
                vmem((2, chunk, ff), bf16),
                vmem((chunk, ff), f32),
                vmem((2, chunk, ff), bf16),
                vmem((slices, 8, 128), f32),
                vmem((models, seqs, 8, 128), f32),
                dma((3,)),
                dma((2,)),
                dma((2,)),
                dma((PIECES,)),
                dma((PIECES,)),
                dma((models, seqs, 1 + seqs // CORES)),
                dma((models, seqs)),
                dma((models, seqs)),
                dma((models, seqs)),
                dma((slices,)),
                dma((slices,)),
                dma((models, seqs)),
                dma((models, seqs)),
            ],
            compiler_params=pltpu.CompilerParams(
                collective_id=0, has_side_effects=True, vmem_limit_bytes=58 * 2**20
            ),
        )(activations[0], gate_pre[0], hidden_grad[0], up_weights[0])

    placed = (
        P("mp", "dp", None),
        P("mp", "dp", "tensor"),
        P("mp", "dp", "tensor"),
        P("mp", "dp", "tensor"),
    )
    return jax.shard_map(
        local, mesh=mesh, in_specs=placed, out_specs=P(("dp", "mp"), "tensor"), check_vma=False
    )
```

```python
import functools
import math

import jax
import jax.numpy as jnp
from jax import lax
from jax.experimental import pallas as pl
from jax.experimental.pallas import tpu as pltpu
from jax.sharding import PartitionSpec as P

LEN = 128
CORES = 2
PIECES = 16
AHEAD = 8
clip_ratio = 0.05
fisher_floor = 0.1
f32 = jnp.float32
bf16 = jnp.bfloat16


def kernel(
    sizes, acts_ref, gate_ref, hid_ref, w_ref, out_ref,
    acts, acts_t, gate, hid, cot, cols_in, w_far, w_own, ratio, merged, part, clips,
    load_sem, own_sem, out_sem,
    w_send, w_recv, c_send, c_recv, a_send, a_recv, g_send, g_recv, z_send, z_recv, k_send, k_recv,
):
    models, seqs, slices = sizes
    m, d, t = lax.axis_index("mp"), lax.axis_index("dp"), lax.axis_index("tensor")
    other = 1 - m
    ys = seqs // CORES
    y, core = d // CORES, d % CORES
    mate = y * CORES + (1 - core)
    width, ff = acts.shape[1], gate.shape[1]
    keep = w_far.shape[0]
    piece = keep // PIECES
    chunk = 2 * piece
    chunks = PIECES // 2
    tile = math.gcd(ff, 512)

    def place(where):
        return dict(zip(("mp", "dp", "tensor"), where))

    def push(src, dst, send, recv, where):
        return pltpu.make_async_remote_copy(
            src_ref=src, dst_ref=dst, send_sem=send, recv_sem=recv,
            device_id=place(where), device_id_type=pl.DeviceIdType.MESH,
        )

    def rest(offset):
        return [(a, b) for a in range(models) for b in range(seqs) if a or b][offset:]

    def plane(a, b):
        return lax.rem(m + a, models), lax.rem(d + b, seqs)

    loads = [
        pltpu.make_async_copy(src, dst, load_sem.at[i])
        for i, (src, dst) in enumerate(((gate_ref, gate), (hid_ref, hid), (acts_ref, acts)))
    ]
    for copy in loads:
        copy.start()

    barrier = pltpu.get_barrier_semaphore()
    for a, b in rest(0):
        pm, pd = plane(a, b)
        pl.semaphore_signal(barrier, inc=1, device_id=place((pm, pd, t)), device_id_type=pl.DeviceIdType.MESH)
    for o in range(1, slices):
        pl.semaphore_signal(
            barrier, inc=1, device_id=place((m, d, lax.rem(t + o, slices))), device_id_type=pl.DeviceIdType.MESH
        )
    pl.semaphore_wait(barrier, models * seqs - 1 + slices - 1)

    def w_piece(k):
        return push(
            w_ref.at[pl.ds(pl.multiple_of(other * keep + k * piece, piece), piece), :],
            w_far.at[pl.ds(pl.multiple_of(k * piece, piece), piece), :],
            w_send.at[k], w_recv.at[k], (other, d, t),
        )

    for k in range(2):
        w_piece(k).start()

    def own_chunk(i):
        slot = lax.rem(i, 2)
        return pltpu.make_async_copy(
            w_ref.at[pl.ds(pl.multiple_of(m * keep + i * chunk, chunk), chunk), :],
            w_own.at[slot], own_sem.at[slot],
        )

    own_chunk(0).start()

    loads[0].wait()
    loads[1].wait()

    @pl.loop(0, ff // tile)
    def _(j):
        at = pl.ds(pl.multiple_of(j * tile, tile), tile)
        v = gate[:, at].astype(f32)
        cot[m, d, :, at] = (hid[:, at].astype(f32) * (v / (1.0 + jnp.exp(-v)))).astype(bf16)

    def cot_to(cm, cs, kind, where):
        return push(cot.at[cm, cs], cot.at[cm, cs], c_send.at[cm, cs, kind], c_recv.at[cm, cs], where)

    def along_y(cm, cs):
        return [cot_to(cm, cs, 1 + o, (m, lax.rem(y + o, ys) * CORES + core, t)) for o in range(1, ys)]

    across = cot_to(m, d, 0, (other, d, t))
    first = [across] + along_y(m, d) + [cot_to(m, d, 1, (m, mate, t))]
    for copy in first:
        copy.start()

    loads[2].wait()
    step = math.gcd(width, 512)

    @pl.loop(0, width // step)
    def _(j):
        at = pl.ds(pl.multiple_of(j * step, step), step)
        acts_t[at, :] = acts[:, at].T

    sub = keep // slices

    def block(bm, bd):
        return acts_t.at[pl.ds(pl.multiple_of((bd * models + bm) * keep, keep), keep), :]

    def rows_of(a, b, sm, sd):
        pm, pd = plane(a, b)
        if a == 0:
            return push(block(pm, pd), cols_in.at[sm, sd], a_send.at[a, b], a_recv.at[sm, sd], (pm, pd, t))
        mine = pl.ds(pl.multiple_of(t * sub, sub), sub)
        return push(
            block(pm, pd).at[mine, :], cols_in.at[sm, sd, mine, :], a_send.at[a, b], a_recv.at[sm, sd], (pm, pd, t)
        )

    def shared(part_of, o):
        at = pl.ds(pl.multiple_of(part_of * sub, sub), sub)
        ref = cols_in.at[other, :, at, :]
        return push(ref, ref, g_send.at[o], g_recv.at[part_of], (m, d, lax.rem(t + o, slices)))

    blocks = [rows_of(a, b, m, d) for a, b in rest(0)]
    for copy in blocks:
        copy.start()
    for k in range(2, 4):
        w_piece(k).start()
    cols_in[m, d] = block(m, d)[...]

    def gram(ref, lead, size):
        deep = math.gcd(size, 1024)

        def add(j, total):
            at = pl.ds(pl.multiple_of(j * deep, deep), deep)
            x = ref[:, at] if lead is None else ref[lead[0], lead[1], :, at]
            return total + lax.dot_general(x, x, (((1,), (1,)), ((), ())), preferred_element_type=f32)

        return lax.fori_loop(0, size // deep, add, jnp.zeros((LEN, LEN), f32))

    share = jnp.sum(gram(acts, None, width) * gram(cot, (m, d), ff), axis=(0, 1), keepdims=True)
    part[t] = jnp.broadcast_to(share, part.shape[1:])
    shares = [
        push(part.at[t], part.at[t], z_send.at[o], z_recv.at[t], (m, d, lax.rem(t + o, slices)))
        for o in range(1, slices)
    ]
    for copy in shares:
        copy.start()
    for o in range(1, slices):
        f = lax.rem(t + o, slices)
        push(part.at[f], part.at[f], z_send.at[o], z_recv.at[f], (m, d, f)).wait_recv()
    norm = jnp.sqrt(jnp.sum(part[...], axis=0))
    limit = clip_ratio * math.sqrt(LEN * width * ff * slices)
    factor = limit / jnp.maximum(norm, limit)
    clips[m, d] = factor * factor
    factors = []
    for a, b in rest(0):
        pm, pd = plane(a, b)
        factors.append(push(clips.at[m, d], clips.at[m, d], k_send.at[a, b], k_recv.at[m, d], (pm, pd, t)))
    for copy in factors:
        copy.start()

    def arrived(cm, cs):
        cot_to(cm, cs, 0, (other, d, t)).wait_recv()

    arrived(other, d)
    second = along_y(other, d) + [cot_to(other, d, 1, (m, mate, t))]
    for copy in second:
        copy.start()
    for k in range(4, AHEAD):
        w_piece(k).start()
    for a, b in rest(0):
        if a:
            rows_of(a, b, *plane(a, b)).wait_recv()
    passed = [shared(t, o) for o in range(1, slices)]
    for copy in passed:
        copy.start()
    third = []
    for cm in (m, other):
        for o in range(1, ys):
            cs = lax.rem(y + o, ys) * CORES + core
            arrived(cm, cs)
            copy = cot_to(cm, cs, 1, (m, mate, t))
            copy.start()
            third.append(copy)
    for cm in (m, other):
        for o in range(ys):
            arrived(cm, lax.rem(y + o, ys) * CORES + (1 - core))
    for a, b in rest(0):
        pm, pd = plane(a, b)
        if a == 0:
            rows_of(a, b, pm, pd).wait_recv()
        push(clips.at[pm, pd], clips.at[pm, pd], k_send.at[a, b], k_recv.at[pm, pd], (pm, pd, t)).wait_recv()

    for o in range(1, slices):
        shared(lax.rem(t + o, slices), o).wait_recv()

    def out_chunk(i):
        slot = lax.rem(i, 2)
        return pltpu.make_async_copy(
            merged.at[slot], out_ref.at[pl.ds(pl.multiple_of(i * chunk, chunk), chunk), :], out_sem.at[slot]
        )

    @pl.loop(0, chunks)
    def _(i):
        slot = lax.rem(i, 2)
        rows = pl.ds(pl.multiple_of(i * chunk, chunk), chunk)

        @pl.when(i >= 1)
        def _():
            w_piece(2 * i - 2).wait_send()
            w_piece(2 * i - 1).wait_send()

        @pl.when((2 * i + 2 >= AHEAD) & (2 * i + 2 < PIECES))
        def _():
            w_piece(2 * i + 2).start()
            w_piece(2 * i + 3).start()

        @pl.when(i + 1 < chunks)
        def _():
            own_chunk(i + 1).start()

        @pl.loop(0, ff // tile)
        def _(j):
            at = pl.ds(pl.multiple_of(j * tile, tile), tile)

            def weight(fm):
                total = jnp.full((chunk, tile), fisher_floor, f32)
                fisher = None
                for s in range(seqs):
                    grad = jnp.dot(cols_in[fm, s, rows, :], cot[fm, s, :, at], preferred_element_type=f32)
                    term = clips[fm, s, 0:1, 0:1] * (grad * grad)
                    fisher = term if fisher is None else fisher + term
                return fisher + total

            far = weight(other)
            ratio[:, at] = far / (far + weight(m))

        own_chunk(i).wait()

        @pl.when(i >= 2)
        def _():
            out_chunk(i - 2).wait()

        for half in range(2):
            w_piece(2 * i + half).wait_recv()
            part_rows = pl.ds(half * piece, piece)
            far_rows = pl.ds(pl.multiple_of(i * chunk + half * piece, piece), piece)

            @pl.loop(0, ff // tile)
            def _(j):
                at = pl.ds(pl.multiple_of(j * tile, tile), tile)
                near = w_own[slot, part_rows, at].astype(f32)
                far = w_far[far_rows, at].astype(f32)
                merged[slot, part_rows, at] = (near + ratio[part_rows, at] * (far - near)).astype(bf16)

        out_chunk(i).start()

    for k in range(PIECES - 2, PIECES):
        w_piece(k).wait_send()
    for copy in first + second + third + blocks + passed + shares + factors:
        copy.wait_send()
    for i in range(chunks - 2, chunks):
        out_chunk(i).wait()


def solution(mesh):
    models, seqs, slices = mesh.shape["mp"], mesh.shape["dp"], mesh.shape["tensor"]

    def local(activations, gate_pre, hidden_grad, up_weights):
        tokens, width = activations.shape[1:]
        ff = gate_pre.shape[2]
        keep = up_weights.shape[1] // models
        chunk = keep // PIECES * 2
        assert tokens == LEN and models == 2 and seqs % CORES == 0
        dma, vmem = pltpu.SemaphoreType.DMA, pltpu.VMEM
        return pl.pallas_call(
            functools.partial(kernel, (models, seqs, slices)),
            out_shape=jax.ShapeDtypeStruct((keep, ff), bf16),
            in_specs=[pl.BlockSpec(memory_space=pl.ANY)] * 4,
            out_specs=pl.BlockSpec(memory_space=pl.ANY),
            scratch_shapes=[
                vmem((LEN, width), bf16),
                vmem((width, LEN), bf16),
                vmem((LEN, ff), bf16),
                vmem((LEN, ff), bf16),
                vmem((models, seqs, LEN, ff), bf16),
                vmem((models, seqs, keep, LEN), bf16),
                vmem((keep, ff), bf16),
                vmem((2, chunk, ff), bf16),
                vmem((chunk, ff), f32),
                vmem((2, chunk, ff), bf16),
                vmem((slices, 8, 128), f32),
                vmem((models, seqs, 8, 128), f32),
                dma((3,)),
                dma((2,)),
                dma((2,)),
                dma((PIECES,)),
                dma((PIECES,)),
                dma((models, seqs, 1 + seqs // CORES)),
                dma((models, seqs)),
                dma((models, seqs)),
                dma((models, seqs)),
                dma((slices,)),
                dma((slices,)),
                dma((slices,)),
                dma((slices,)),
                dma((models, seqs)),
                dma((models, seqs)),
            ],
            compiler_params=pltpu.CompilerParams(
                collective_id=0, has_side_effects=True, vmem_limit_bytes=58 * 2**20
            ),
        )(activations[0], gate_pre[0], hidden_grad[0], up_weights[0])

    placed = (
        P("mp", "dp", None),
        P("mp", "dp", "tensor"),
        P("mp", "dp", "tensor"),
        P("mp", "dp", "tensor"),
    )
    return jax.shard_map(
        local, mesh=mesh, in_specs=placed, out_specs=P(("dp", "mp"), "tensor"), check_vma=False
    )
```
